128 devices in a mesh: dp: 16 (over x, y), row: 2 (over z_hi), col: 4 (over z_lo, core).
Axes of the slice: x: 4, y: 4, z: 4 (z_hi: 2, z_lo: 2; z = z_hi * 2 + z_lo), core: 2. Of those that a mesh axis runs over, the one named last changes fastest.
Arguments:
- act_in: bfloat16 [16384, 768], P(('dp', 'col'), 'row'), may hold values from -6 to 6
- cotangent: bfloat16 [16384, 768], P(('dp', 'col'), 'row'), may hold values from -6 to 6
- lengths: int32 [16], P('dp'), may hold values from 769 to 1024, as said below
- w_qkv: bfloat16 [2, 768, 3, 768], P(None, 'row', None, 'col'), may hold values from -0.21875 to 0.21875
- bias_qv: bfloat16 [2, 2, 768], P(None, None, 'col'), may hold values from -0.75 to 0.75
- w_out: bfloat16 [2, 768, 768], P(None, 'col', 'row'), may hold values from -4 to 4
- bias_out: bfloat16 [2, 768], P(None, 'row'), may hold values from -4 to 4
- w_up: bfloat16 [2, 768, 3072], P(None, 'row', 'col'), may hold values from -0.21875 to 0.21875
- bias_up: bfloat16 [2, 3072], P(None, 'col'), may hold values from -4 to 4
- w_down: bfloat16 [2, 3072, 768], P(None, 'col', 'row'), may hold values from -0.109375 to 0.109375
- bias_down: bfloat16 [2, 768], P(None, 'row'), may hold values from -4 to 4
- ln_gain: bfloat16 [2, 2, 768], P(None, None, 'row'), may hold values from 0.3 to 2
- ln_shift: bfloat16 [2, 2, 768], P(None, None, 'row'), may hold values from -4 to 4
Outputs:
- out_act: bfloat16 [16384, 768], P(('dp', 'col'), 'row')
- grad_in: float32 [16384, 768], P(('dp', 'col'), 'row')
- grad_qkv: float32 [2, 768, 3, 768], P(None, 'row', None, 'col')
- grad_bias_qv: float32 [2, 2, 768], P(None, None, 'col')
- grad_out_proj: float32 [2, 768, 768], P(None, 'col', 'row')
- grad_out_bias: float32 [2, 768], P(None, 'row')
- grad_up: float32 [2, 768, 3072], P(None, 'row', 'col')
- grad_up_bias: float32 [2, 3072], P(None, 'col')
- grad_down: float32 [2, 3072, 768], P(None, 'col', 'row')
- grad_down_bias: float32 [2, 768], P(None, 'row')
- grad_gain: float32 [2, 2, 768], P(None, None, 'row')
- grad_shift: float32 [2, 2, 768], P(None, None, 'row')
The draws below stay inside these ranges and needn't reach their ends.
Inputs may be any that keep to these rules, and one draw needn't show every extreme that they name: `lengths`: each group's valid tokens form one sequence at the start of its buffer; at least one group in every draw is completely filled.
All inputs are finite; a program needn't handle non-finite values.
Results may differ from the reference program's by a relative error of at most 0.013.
Values may be sent and summed in bfloat16 or wider, within the bound.
No kernel may reach another device: no remote copies, remote signals or barrier semaphores. Data moves between devices by JAX's collectives and lax.ppermute only.
A program may use at most 128 MiB of HBM per device.

```python
import jax
import jax.numpy as jnp
from jax import lax

D = 768
HEADS = 12
HDIM = 64
FF = 3072
LAYERS = 2
GROUP_TOK = 1024
TOKENS = 16384
N_DP = 16


def draw_lengths(key, part):
    key = jax.random.fold_in(key, 11)
    first, second = jax.random.split(key)
    drawn = jax.random.randint(first, (N_DP,), 3 * GROUP_TOK // 4 + 1, GROUP_TOK + 1)
    fullest = jax.random.randint(second, (), 0, N_DP)
    return jnp.where(jnp.arange(N_DP) == fullest, GROUP_TOK, drawn).astype(jnp.int32)


def feature_ramp(low_end, high_end):
    place = jnp.arange(D, dtype=jnp.float32) / (D - 1)
    return low_end * (high_end / low_end) ** place


def draw_cotangent(key, part):
    key = jax.random.fold_in(key, 23)
    first, second = jax.random.split(key)
    noise = jax.random.normal(first, (TOKENS, D), jnp.float32)
    ramp = feature_ramp(0.5, 1.5)
    common = 0.3 * jax.random.uniform(second, (TOKENS, 1), jnp.float32, 0.5, 1.5)
    value = ramp[None, :] * (noise + common)
    return jnp.clip(value, -6.0, 6.0).astype(jnp.bfloat16)


def draw_ln_gain(key, part):
    key = jax.random.fold_in(key, 37)
    rough = jax.random.uniform(key, (LAYERS, 2, D), jnp.float32, 0.8, 1.2)
    ramp = feature_ramp(0.5, 1.5)
    return jnp.clip(ramp[None, None, :] * rough, 0.3, 2.0).astype(jnp.bfloat16)


def level_of(own_key, dims, shards, smallest, largest):
    level = 1.0
    for position, blocks in shards:
        steps = jax.random.uniform(jax.random.fold_in(jax.random.fold_in(own_key, 6), position), (blocks,), jnp.float32, smallest / len(shards), largest / len(shards))
        level = level * jnp.repeat(jnp.exp(steps), dims[position] // blocks).reshape((-1,) + (1,) * (len(dims) - 1 - position))
    return level


def normal_values(key, shape, deviation, reach, cuts=(), kind=jnp.bfloat16):
    level = level_of(key, shape, cuts, -0.22, 0.18) if cuts else 1.0
    values = jax.random.normal(key, shape, jnp.float32) * deviation * level
    return jnp.minimum(jnp.maximum(values, -reach), reach).astype(kind)


def setup_inputs(seed: int = 0) -> dict:
    splits = jax.random.split(jax.random.key(seed), 14)
    return {
        "act_in": normal_values(splits[0], (TOKENS, D), 1.0, 6.0, ((0, 64), (1, 2))),
        "cotangent": draw_cotangent(jax.random.fold_in(splits[13], 71), 0),
        "lengths": draw_lengths(jax.random.fold_in(splits[13], 71), 0),
        "w_qkv": normal_values(splits[3], (LAYERS, D, 3, D), D ** -0.5, 0.21875, ((1, 2), (3, 4))),
        "bias_qv": normal_values(splits[4], (LAYERS, 2, D), 0.05, 0.75, ((2, 4),)),
        "w_out": normal_values(splits[5], (LAYERS, D, D), (max(1, 3 * D // GROUP_TOK)) ** -0.5, 4.0, ((1, 4), (2, 2))),
        "bias_out": normal_values(splits[6], (LAYERS, D), 0.3, 4.0, ((1, 2),)),
        "w_up": normal_values(splits[7], (LAYERS, D, FF), D ** -0.5, 0.21875, ((1, 2), (2, 4))),
        "bias_up": normal_values(splits[8], (LAYERS, FF), 0.3, 4.0, ((1, 4),)),
        "w_down": normal_values(splits[9], (LAYERS, FF, D), FF ** -0.5, 0.109375, ((1, 4), (2, 2))),
        "bias_down": normal_values(splits[10], (LAYERS, D), 0.3, 4.0, ((1, 2),)),
        "ln_gain": draw_ln_gain(jax.random.fold_in(splits[13], 71), 0),
        "ln_shift": normal_values(splits[12], (LAYERS, 2, D), 0.3, 4.0, ((2, 2),)),
    }


@jax.custom_vjp
def low(v):
    return lax.optimization_barrier(v.astype(jnp.bfloat16)).astype(jnp.float32)

@jax.custom_vjp
def low_back(v):
    return v

def low_keep(v):
    return (low(v), None)

def low_pass(kept, grad):
    return (grad,)

def back_keep(v):
    return (v, None)

def back_low(kept, grad):
    return (low(grad),)
low.defvjp(low_keep, low_pass)
low_back.defvjp(back_keep, back_low)

def norm_rows(resid, gain, shift):
    mean = lax.optimization_barrier(jnp.mean(resid, axis=-1, keepdims=True))
    square = lax.optimization_barrier(jnp.mean(resid * resid, axis=-1, keepdims=True))
    inverse = lax.rsqrt(square - mean * mean + 1e-05)
    return (resid - mean) * inverse * gain + shift

def attend(query, keys, values, key_ok):
    block_rows = min(512, GROUP_TOK)
    blocks = query.reshape(GROUP_TOK // block_rows, block_rows, HEADS, HDIM)

    def single_block(query_block):
        scores = jnp.einsum('qhd,khd->hqk', query_block, keys, precision=lax.Precision.HIGHEST) * 0.125
        scores = low_back(scores)
        scores = jnp.where(key_ok[None, None, :], scores, -1000000000.0)
        probs = low(jax.nn.softmax(scores, axis=2))
        return jnp.einsum('hqk,khd->qhd', probs, values, precision=lax.Precision.HIGHEST)
    mixture = lax.map(jax.checkpoint(single_block), blocks)
    return mixture.reshape(GROUP_TOK, HEADS * HDIM)

def layer_forward(state, w_qkv, bias_qv, w_out, bias_out, w_up, bias_up, w_down, bias_down, gain, shift, key_ok):
    high = lax.Precision.HIGHEST
    rounded = low(state)
    qkv = jnp.einsum('ta,asc->tsc', rounded, w_qkv, precision=high)
    qkv = qkv + jnp.stack([bias_qv[0], jnp.zeros_like(bias_qv[0]), bias_qv[1]])[None]
    qkv = low(low_back(qkv))
    query = qkv[:, 0].reshape(GROUP_TOK, HEADS, HDIM)
    keys = qkv[:, 1].reshape(GROUP_TOK, HEADS, HDIM)
    values = qkv[:, 2].reshape(GROUP_TOK, HEADS, HDIM)
    mixture = low(low_back(attend(query, keys, values, key_ok)))
    branch = low_back(jnp.dot(mixture, w_out, precision=high) + bias_out)
    normed = norm_rows(state + branch, gain[0], shift[0])
    hidden_pre = low_back(jnp.dot(low(normed), w_up, precision=high) + bias_up)
    hidden = low(jax.nn.gelu(hidden_pre, approximate=False))
    branch_two = low_back(jnp.dot(hidden, w_down, precision=high) + bias_down)
    return norm_rows(normed + branch_two, gain[1], shift[1])

def reference(act_in, cotangent, lengths, w_qkv, bias_qv, w_out, bias_out, w_up, bias_up, w_down, bias_down, ln_gain, ln_shift):
    weights = tuple((w.astype(jnp.float32) for w in (w_qkv, bias_qv, w_out, bias_out, w_up, bias_up, w_down, bias_down, ln_gain, ln_shift)))
    inputs = act_in.astype(jnp.float32).reshape(N_DP, GROUP_TOK, D)
    grads_out = cotangent.astype(jnp.float32).reshape(N_DP, GROUP_TOK, D)

    def group_step(totals, item):
        state, grad_out, length = item
        key_ok = jnp.arange(GROUP_TOK, dtype=jnp.int32) < length

        def run(start, *params):
            value = start
            for layer in range(LAYERS):
                value = layer_forward(value, *[p[layer] for p in params], key_ok)
            return value
        result, pull = jax.vjp(run, state, *weights)
        grads = pull(jnp.where(key_ok[:, None], grad_out, 0.0))
        output = jnp.where(key_ok[:, None], result, 0.0).astype(jnp.bfloat16)
        totals = tuple((t + g for t, g in zip(totals, grads[1:])))
        return (totals, (output, grads[0]))
    start_totals = tuple((jnp.zeros_like(w) for w in weights))
    totals, (outputs, input_grads) = lax.scan(group_step, start_totals, (inputs, grads_out, lengths))
    return (outputs.reshape(TOKENS, D), input_grads.reshape(TOKENS, D), totals[0], totals[1], totals[2], totals[3], totals[4], totals[5], totals[6], totals[7], totals[8], totals[9])
```

```python
import jax
import jax.numpy as jnp
from jax import lax
from jax.sharding import Mesh
from jax.sharding import PartitionSpec as P

LAYERS = 2
HDIM = 64
HEADS = 6
GROUP = 1024
QUARTER = 256
WIDTH = 768
HALF = 384
BLOCK = 192
HID = 768
PACK_A = 768
PACK_B = 1536
SMALL = 456

EPSILON = 1e-05
MASKED = -1000000000.0

LINE = ("row", "zl")
PLANE = ("x", "y")
bf16 = jnp.bfloat16
f32 = jnp.float32


def swapped(value, axes, count, bits):
    return lax.ppermute(value, axes, [(i, i ^ bits) for i in range(count)])


def in_order(parts, place):
    flip = (place % 2) == 1
    parts = [jnp.where(flip, parts[s ^ 1], parts[s]) for s in range(4)]
    flip = (place // 2) == 1
    return [jnp.where(flip, parts[s ^ 2], parts[s]) for s in range(4)]


def gather(value, axes):
    return [value] + [swapped(value, axes, 4, bits) for bits in (1, 3, 2)]


def near_first(parts):
    return [parts[0], parts[1], parts[3], parts[2]]


def piece_of(value, index, dim):
    return lax.dynamic_index_in_dim(value, index, dim, keepdims=False)


def split3(value):
    high = lax.reduce_precision(value, 8, 7)
    rest = value - high
    middle = lax.reduce_precision(rest, 8, 7)
    return jnp.stack([high, middle, rest - middle]).astype(bf16)


def dot(left, right, dims):
    return lax.dot_general(left, right, ((dims[0], dims[1]), ((), ())), preferred_element_type=f32)


def mm(left, right):
    return dot(left, right, ((1,), (0,)))


def mt(left, right):
    return dot(left, right, ((1,), (1,)))


def tm(left, right):
    return dot(left, right, ((0,), (0,)))


def core_sum(value):
    return value + swapped(value, "core", 2, 1)


def norm_forward(resid, gain, shift):
    mean = jnp.mean(resid, 1, keepdims=True)
    square = jnp.mean(resid * resid, 1, keepdims=True)
    inverse = lax.rsqrt(square - mean * mean + EPSILON)
    unit = (resid - mean) * inverse
    return unit * gain + shift, unit, inverse


def norm_backward(grad, unit, inverse, gain):
    scaled = grad * gain
    first = jnp.mean(scaled, 1, keepdims=True)
    second = jnp.mean(scaled * unit, 1, keepdims=True)
    resid_grad = inverse * (scaled - first - unit * second)
    return resid_grad, jnp.sum(grad * unit, 0), jnp.sum(grad, 0)


def heads_of(value):
    return value.reshape(value.shape[0], HEADS, HDIM)


def attend_forward(query, keys, values, key_ok):
    scores = jnp.einsum("qhd,khd->hqk", heads_of(query), heads_of(keys), preferred_element_type=f32) * 0.125
    scores = jnp.where(key_ok[None, None, :], scores, MASKED)
    peak = jnp.max(scores, axis=2, keepdims=True)
    raised = jnp.exp(scores - peak)
    probs = raised / jnp.sum(raised, axis=2, keepdims=True)
    mixture = jnp.einsum("hqk,khd->qhd", probs.astype(bf16), heads_of(values), preferred_element_type=f32)
    return mixture.reshape(QUARTER, HEADS * HDIM), probs


def attend_backward(query, keys, values, probs, grad):
    grad = heads_of(grad)
    grad_probs = jnp.einsum("qhd,khd->hqk", grad, heads_of(values), preferred_element_type=f32)
    inner = jnp.sum(probs * grad_probs, axis=2, keepdims=True)
    grad_scores = (probs * (grad_probs - inner)).astype(bf16)
    query_grad = jnp.einsum("hqk,khd->qhd", grad_scores, heads_of(keys), preferred_element_type=f32) * 0.125
    key_grad = jnp.einsum("hqk,qhd->khd", grad_scores, heads_of(query), preferred_element_type=f32) * 0.125
    value_grad = jnp.einsum("hqk,qhd->khd", probs.astype(bf16), grad, preferred_element_type=f32)
    return (
        query_grad.reshape(QUARTER, HEADS * HDIM),
        key_grad.reshape(GROUP, HEADS * HDIM),
        value_grad.reshape(GROUP, HEADS * HDIM),
    )


def gelu_exact(value):
    return jax.nn.gelu(value, approximate=False)


def weight_grad(pairs):
    blocks = []
    for row in range(2):
        for z in range(2):
            blocks += [tm(right[z], left[:, row * HALF : (row + 1) * HALF]).astype(bf16) for left, right in pairs]
    return jnp.concatenate(blocks, 0).reshape(64, -1, HALF)


def plane_pieces(pieces):
    return pieces.reshape(4, 16, -1, HALF).transpose(1, 0, 2, 3).reshape(16, -1, HALF)


def plane_exchange(pieces):
    return lax.all_to_all(pieces, PLANE, 0, 0, tiled=True)


def plane_sum(received):
    return jnp.sum(received, 0, dtype=f32)


def line_sum(pieces, place):
    total = piece_of(pieces, place, 0).astype(f32)
    for bits in (1, 3, 2):
        total = total + swapped(piece_of(pieces, place ^ bits, 0), LINE, 4, bits).astype(f32)
    return total


def exchange(pieces):
    return lax.all_to_all(pieces, LINE + PLANE, 0, 0, tiled=True)


def when(value):
    return lax.slice(value, (0,) * value.ndim, (1,) * value.ndim).reshape(()).astype(f32) * 0.0


def on_device(
    act_in, cotangent, lengths, w_qkv, bias_qv, w_out, bias_out, w_up, bias_up, w_down, bias_down, ln_gain, ln_shift
):
    at_x, at_y = lax.axis_index("x"), lax.axis_index("y")
    row, zl, core = lax.axis_index("row"), lax.axis_index("zl"), lax.axis_index("core")
    place = 2 * row + zl

    first = in_order(near_first(gather(jnp.concatenate([w_qkv[0].reshape(HALF, 3 * BLOCK), w_out[0].T], 1), LINE)), place)
    first = [jnp.concatenate([first[z], first[2 + z]], 0) for z in range(2)]
    rank = 4 * at_x + at_y
    late = [lax.dynamic_slice_in_dim(part, 24 * rank, 24, dim) for part, dim in ((w_qkv, 1), (w_out, 2), (w_up, 1), (w_down, 2))]
    late = [late[0].reshape(LAYERS, 24, 3 * BLOCK), late[1].transpose(0, 2, 1), late[2], late[3].transpose(0, 2, 1)]
    sooner = jnp.concatenate([late[2][0], late[3][0], late[0][1], late[1][1]], 1)
    later = jnp.concatenate([late[2][1], late[3][1]], 1)
    sooner = lax.all_gather(sooner, LINE + PLANE, axis=0, tiled=True).reshape(2, 2, HALF, -1)
    later = lax.all_gather(later, LINE + PLANE, axis=0, tiled=True).reshape(2, 2, HALF, -1)

    def part(late, z, start, count):
        return jnp.concatenate([late[0, z, :, start : start + count], late[1, z, :, start : start + count]], 0)

    weights_a = [first, [part(sooner, z, PACK_B, PACK_A) for z in range(2)]]
    weights_b = [[part(late, z, 0, PACK_B) for z in range(2)] for late in (sooner, later)]

    def both_blocks(value):
        other = swapped(value, "zl", 2, 1)
        pair = jnp.where(zl == 0, jnp.stack([value, other]), jnp.stack([other, value]))
        return jnp.concatenate([pair[0], pair[1]], -1)

    def both_halves(value):
        other = swapped(value, "row", 2, 1)
        pair = jnp.where(row == 0, jnp.stack([value, other]), jnp.stack([other, value]))
        return jnp.concatenate([pair[0], pair[1]], -1)

    column_small = both_blocks(jnp.concatenate([bias_qv.reshape(2, 2 * BLOCK), bias_up], 1)).astype(f32)
    column_small = column_small.reshape(LAYERS, 2, 2 * BLOCK + HID)
    feature_small = jnp.concatenate([bias_out[:, None], bias_down[:, None], ln_gain, ln_shift], 1)
    feature_small = both_halves(feature_small).astype(f32)

    mates = [(2 * z + 1, 4 + 2 * z) for z in range(2)] + [(4 + 2 * z, 2 * z + 1) for z in range(2)]
    everywhere = ("row", "zl", "core")
    at_home = core == row
    entered = jnp.concatenate([act_in, cotangent], 0)
    mine = jnp.where(at_home, entered, lax.ppermute(entered, everywhere, mates))
    other = swapped(mine, "core", 2, 1)
    entered = jnp.where(core == 0, jnp.concatenate([mine, other], 1), jnp.concatenate([other, mine], 1))
    length = lengths[0]
    ones = jnp.arange(QUARTER, dtype=jnp.int32)
    key_at = jnp.concatenate([(2 * (zl ^ (s & 1)) + (row ^ (s >> 1))) * QUARTER + ones for s in (0, 1, 3, 2)])
    key_ok = key_at < length
    own_ok = ((2 * zl + row) * QUARTER + ones < length)[:, None]

    kept = []
    state = entered[:QUARTER].astype(f32)
    for l in range(LAYERS):
        wa, wb = weights_a[l], weights_b[l]
        gain = feature_small[l, 2:4]
        shift = feature_small[l, 4:6]
        low = state.astype(bf16)
        qkv = []
        for z in range(2):
            value = mm(low, wa[z][:, : 3 * BLOCK])
            bias = column_small[l, z]
            bias = jnp.concatenate([bias[:BLOCK], jnp.zeros((BLOCK,), f32), bias[BLOCK : 2 * BLOCK]])
            qkv.append((value + bias).astype(bf16))
        query = jnp.concatenate([qkv[0][:, :BLOCK], qkv[1][:, :BLOCK]], 1)
        key_value = jnp.concatenate(
            [qkv[z][:, s * BLOCK : (s + 1) * BLOCK] for s in (1, 2) for z in range(2)], 1
        )
        key_value = jnp.concatenate(gather(key_value, LINE), 0)
        keys, values = key_value[:, : 2 * BLOCK], key_value[:, 2 * BLOCK :]
        mixture, probs = attend_forward(query, keys, values, key_ok)
        mixture = mixture.astype(bf16)
        branch = sum(mt(mixture[:, z * BLOCK : (z + 1) * BLOCK], wa[z][:, 3 * BLOCK :]) for z in range(2))
        branch = core_sum(branch) + feature_small[l, 0]
        normed, unit_one, inverse_one = norm_forward(state + branch, gain[0], shift[0])
        mix_parts = [mixture[:, z * BLOCK : (z + 1) * BLOCK] for z in range(2)]
        normed_low = normed.astype(bf16)
        pre = [mm(normed_low, wb[z][:, :HID]) + column_small[l, z, 2 * BLOCK :] for z in range(2)]
        hidden = [gelu_exact(pre[z]).astype(bf16) for z in range(2)]
        branch = sum(mt(hidden[z], wb[z][:, HID:]) for z in range(2))
        branch = core_sum(branch) + feature_small[l, 1]
        state, unit_two, inverse_two = norm_forward(normed + branch, gain[1], shift[1])
        kept.append(
            (low, mix_parts, query, keys, values, probs, unit_one, inverse_one, normed_low, pre, hidden, unit_two, inverse_two)
        )

    def to_output(value):
        halves = (value[:, :HALF], value[:, HALF:])
        sent = jnp.where(row == 0, halves[1], halves[0])
        here = jnp.where(row == 0, halves[0], halves[1])
        return jnp.where(at_home, here, lax.ppermute(sent, everywhere, mates))

    output = to_output(jnp.where(own_ok, state, 0.0).astype(bf16))
    grad_state = jnp.where(own_ok, entered[QUARTER:].astype(f32), 0.0)
    wide = []
    narrow = [[], []]
    for l in range(LAYERS - 1, -1, -1):
        low, mix_parts, query, keys, values, probs, unit_one, inverse_one, normed_low, pre, hidden, unit_two, inverse_two = kept[l]
        wa, wb = weights_a[l], weights_b[l]
        gain = feature_small[l, 2:4]
        resid_two, gain_two, shift_two = norm_backward(grad_state, unit_two, inverse_two, gain[1])
        grad_low = resid_two.astype(bf16)
        down_bias = jnp.sum(grad_low, 0, dtype=f32)
        pre_grad = []
        for z in range(2):
            hidden_grad = mm(grad_low, wb[z][:, HID:])
            pre_grad.append(jax.vjp(gelu_exact, pre[z])[1](hidden_grad)[0].astype(bf16))
        up_bias = [jnp.sum(pre_grad[z], 0, dtype=f32) for z in range(2)]
        normed_grad = resid_two + core_sum(sum(mt(pre_grad[z], wb[z][:, :HID]) for z in range(2)))
        pieces = plane_pieces(weight_grad([(normed_low, pre_grad), (grad_low, hidden)]))
        if l == 1:
            one = plane_exchange(pieces)
        else:
            one = line_sum(one.reshape(4, 96, HALF).astype(bf16), place).astype(bf16)
            zero = plane_exchange(jnp.concatenate([pieces, one_a.astype(bf16).reshape(16, 48, HALF)], 1))
        resid_one, gain_one, shift_one = norm_backward(normed_grad, unit_one, inverse_one, gain[0])
        attn_low = resid_one.astype(bf16)
        out_bias = jnp.sum(attn_low, 0, dtype=f32)
        mixture_grad = jnp.concatenate([mm(attn_low, wa[z][:, 3 * BLOCK :]) for z in range(2)], 1).astype(bf16)
        query_grad, key_grad, value_grad = attend_backward(query, keys, values, probs, mixture_grad)
        key_value_grad = jnp.concatenate([key_grad, value_grad], 1).reshape(4, QUARTER, 4 * BLOCK)
        parts = [swapped(key_value_grad[i].astype(bf16), LINE, 4, bits) for i, bits in ((1, 1), (2, 3), (3, 2))]
        key_value_grad = key_value_grad[0] + sum(part.astype(f32) for part in parts)
        if l == 0:
            key_value_grad = key_value_grad + when(one)
            one = lax.all_gather(one, PLANE, axis=0, tiled=True)
        qkv_grad = []
        for z in range(2):
            cut = slice(z * BLOCK, (z + 1) * BLOCK)
            later = slice((z + 2) * BLOCK, (z + 3) * BLOCK)
            qkv_grad.append(
                jnp.concatenate([query_grad[:, cut], key_value_grad[:, cut], key_value_grad[:, later]], 1).astype(bf16)
            )
        qkv_bias = [jnp.sum(qkv_grad[z], 0, dtype=f32) for z in range(2)]
        grad_state = resid_one + core_sum(sum(mt(qkv_grad[z], wa[z][:, : 3 * BLOCK]) for z in range(2)))
        full_a = weight_grad([(low, qkv_grad), (attn_low, mix_parts)])
        if l == 1:
            one = plane_sum(one)
            grad_state = grad_state + when(one)
            one_a = line_sum(full_a.reshape(4, PACK_A, HALF), place)
        else:
            zero = plane_sum(zero) + when(one)
        wide += [out_bias, down_bias, gain_one, gain_two, shift_one, shift_two]
        narrow = [narrow[z] + [qkv_bias[z], up_bias[z]] for z in range(2)]

    grad_in = to_output(grad_state)

    wide = jnp.stack(wide) + when(zero)
    narrow = [jnp.concatenate(part) for part in narrow]
    small = jnp.stack(
        [jnp.concatenate([wide[:, (j // 2) * HALF : (j // 2 + 1) * HALF].reshape(-1), narrow[j % 2]]) for j in range(4)]
    )
    small = split3(small.reshape(4, 16, SMALL)).transpose(1, 2, 0, 3).reshape(4, 16, 3 * SMALL)
    small = jnp.pad(small, ((0, 0), (0, 0), (0, 8 * HALF - 3 * SMALL))).reshape(64, 8, HALF)
    moved = exchange(jnp.concatenate([full_a, small], 1))
    zero_b = line_sum(zero[:HALF].reshape(4, 96, HALF).astype(bf16), place).astype(bf16)
    own = jnp.sum(moved[:, 48:].reshape(64, 8 * HALF)[:, : 3 * SMALL].reshape(64 * 3, SMALL), 0, dtype=f32)
    own = jnp.pad(split3(own).reshape(-1), (0, 8 * HALF - 3 * SMALL)).reshape(8, HALF)
    zero = jnp.concatenate([zero_b, zero[HALF:].astype(bf16), jnp.sum(moved[:, :48], 0, dtype=f32).astype(bf16), own], 0)
    zero = jnp.stack(in_order(near_first(gather(zero, "y")), at_y))
    zero = jnp.stack(in_order(near_first(gather(zero, "x")), at_x)).reshape(16, 200, HALF)
    own = zero[:, 192:].reshape(16, 8 * HALF)[:, : 3 * SMALL].reshape(16, 3, SMALL).astype(f32)
    own = jnp.sum(own, 1).reshape(-1)
    wide = own[: 12 * HALF].reshape(LAYERS, 6, HALF)[::-1]
    own = own[12 * HALF :].reshape(LAYERS, 3 * BLOCK + HID)[::-1]
    grad_a = [zero[:, 144:192].reshape(PACK_A, HALF), zero[:, 96:144].reshape(PACK_A, HALF)]
    grad_b = [zero[:, :96].reshape(PACK_B, HALF), one.reshape(PACK_B, HALF)]

    def both(parts, turn):
        return jnp.stack([part.T if turn else part for part in parts]).astype(f32)

    return (
        output,
        grad_in,
        both([part[: 3 * BLOCK] for part in grad_a], True).reshape(LAYERS, HALF, 3, BLOCK),
        jnp.stack([own[:, :BLOCK], own[:, 2 * BLOCK : 3 * BLOCK]], 1),
        both([part[3 * BLOCK :] for part in grad_a], False),
        wide[:, 0],
        both([part[:HID] for part in grad_b], True),
        own[:, 3 * BLOCK :],
        both([part[HID:] for part in grad_b], False),
        wide[:, 1],
        wide[:, 2:4],
        wide[:, 4:6],
    )


def solution(mesh):
    fine = Mesh(mesh.devices.reshape(4, 4, 2, 2, 2), ("x", "y", "row", "zl", "core"))
    tokens = P(("x", "y", "zl", "core"), "row")
    col = ("zl", "core")
    in_specs = (
        tokens,
        tokens,
        P(("x", "y")),
        P(None, "row", None, col),
        P(None, None, col),
        P(None, col, "row"),
        P(None, "row"),
        P(None, "row", col),
        P(None, col),
        P(None, col, "row"),
        P(None, "row"),
        P(None, None, "row"),
        P(None, None, "row"),
    )
    out_specs = (tokens, tokens) + in_specs[3:8] + (in_specs[8],) + in_specs[9:11] + (in_specs[11], in_specs[12])
    return jax.shard_map(on_device, mesh=fine, in_specs=in_specs, out_specs=out_specs, check_vma=False)
```

```python
import jax
import jax.numpy as jnp
from jax import lax
from jax.sharding import Mesh
from jax.sharding import PartitionSpec as P

LAYERS = 2
HDIM = 64
HEADS = 6
GROUP = 1024
QUARTER = 256
WIDTH = 768
HALF = 384
BLOCK = 192
HID = 768
PACK_A = 768
PACK_B = 1536
SMALL = 19

EPSILON = 1e-05
MASKED = -1000000000.0

LINE = ("row", "zl")
PLANE = ("x", "y")
bf16 = jnp.bfloat16
f32 = jnp.float32


def swapped(value, axes, count, bits):
    return lax.ppermute(value, axes, [(i, i ^ bits) for i in range(count)])


def in_order(parts, place):
    flip = (place % 2) == 1
    parts = [jnp.where(flip, parts[s ^ 1], parts[s]) for s in range(4)]
    flip = (place // 2) == 1
    return [jnp.where(flip, parts[s ^ 2], parts[s]) for s in range(4)]


def gather(value, axes):
    return [value] + [swapped(value, axes, 4, bits) for bits in (1, 3, 2)]


def near_first(parts):
    return [parts[0], parts[1], parts[3], parts[2]]


def piece_of(value, index, dim):
    return lax.dynamic_index_in_dim(value, index, dim, keepdims=False)


def split3(value):
    high = lax.reduce_precision(value, 8, 7)
    rest = value - high
    middle = lax.reduce_precision(rest, 8, 7)
    return jnp.stack([high, middle, rest - middle]).astype(bf16)


def dot(left, right, dims):
    return lax.dot_general(left, right, ((dims[0], dims[1]), ((), ())), preferred_element_type=f32)


def mm(left, right):
    return dot(left, right, ((1,), (0,)))


def mt(left, right):
    return dot(left, right, ((1,), (1,)))


def tm(left, right):
    return dot(left, right, ((0,), (0,)))


def core_sum(value):
    return value + swapped(value, "core", 2, 1)


def norm_forward(resid, gain, shift):
    mean = jnp.mean(resid, 1, keepdims=True)
    square = jnp.mean(resid * resid, 1, keepdims=True)
    inverse = lax.rsqrt(square - mean * mean + EPSILON)
    unit = (resid - mean) * inverse
    return unit * gain + shift, unit, inverse


def norm_backward(grad, unit, inverse, gain):
    scaled = grad * gain
    first = jnp.mean(scaled, 1, keepdims=True)
    second = jnp.mean(scaled * unit, 1, keepdims=True)
    resid_grad = inverse * (scaled - first - unit * second)
    return resid_grad, jnp.sum(grad * unit, 0), jnp.sum(grad, 0)


def heads_of(value):
    return value.reshape(value.shape[0], HEADS, HDIM)


def attend_forward(query, keys, values, key_ok):
    scores = jnp.einsum("qhd,khd->hqk", heads_of(query), heads_of(keys), preferred_element_type=f32) * 0.125
    scores = jnp.where(key_ok[None, None, :], scores, MASKED)
    peak = jnp.max(scores, axis=2, keepdims=True)
    raised = jnp.exp(scores - peak)
    probs = raised / jnp.sum(raised, axis=2, keepdims=True)
    mixture = jnp.einsum("hqk,khd->qhd", probs.astype(bf16), heads_of(values), preferred_element_type=f32)
    return mixture.reshape(QUARTER, HEADS * HDIM), probs


def attend_backward(query, keys, values, probs, grad):
    grad = heads_of(grad)
    grad_probs = jnp.einsum("qhd,khd->hqk", grad, heads_of(values), preferred_element_type=f32)
    inner = jnp.sum(probs * grad_probs, axis=2, keepdims=True)
    grad_scores = (probs * (grad_probs - inner)).astype(bf16)
    query_grad = jnp.einsum("hqk,khd->qhd", grad_scores, heads_of(keys), preferred_element_type=f32) * 0.125
    key_grad = jnp.einsum("hqk,qhd->khd", grad_scores, heads_of(query), preferred_element_type=f32) * 0.125
    value_grad = jnp.einsum("hqk,qhd->khd", probs.astype(bf16), grad, preferred_element_type=f32)
    return (
        query_grad.reshape(QUARTER, HEADS * HDIM),
        key_grad.reshape(GROUP, HEADS * HDIM),
        value_grad.reshape(GROUP, HEADS * HDIM),
    )


def gelu_exact(value):
    return jax.nn.gelu(value, approximate=False)


def weight_grad(pairs):
    blocks = []
    for row in range(2):
        for z in range(2):
            blocks += [tm(right[z], left[:, row * HALF : (row + 1) * HALF]).astype(bf16) for left, right in pairs]
    return jnp.concatenate(blocks, 0).reshape(64, -1, HALF)


def plane_pieces(pieces):
    return pieces.reshape(4, 16, -1, HALF).transpose(1, 0, 2, 3).reshape(16, -1, HALF)


def plane_exchange(pieces):
    return lax.all_to_all(pieces, PLANE, 0, 0, tiled=True)


def plane_sum(received):
    return jnp.sum(received, 0, dtype=f32)


def line_sum(pieces, place):
    total = piece_of(pieces, place, 0).astype(f32)
    for bits in (1, 3, 2):
        total = total + swapped(piece_of(pieces, place ^ bits, 0), LINE, 4, bits).astype(f32)
    return total


def when(value):
    return lax.slice(value, (0,) * value.ndim, (1,) * value.ndim).reshape(()).astype(f32) * 0.0


def on_device(
    act_in, cotangent, lengths, w_qkv, bias_qv, w_out, bias_out, w_up, bias_up, w_down, bias_down, ln_gain, ln_shift
):
    at_x, at_y = lax.axis_index("x"), lax.axis_index("y")
    row, zl, core = lax.axis_index("row"), lax.axis_index("zl"), lax.axis_index("core")
    place = 2 * row + zl

    first = in_order(near_first(gather(jnp.concatenate([w_qkv[0].reshape(HALF, 3 * BLOCK), w_out[0].T], 1), LINE)), place)
    first = [jnp.concatenate([first[z], first[2 + z]], 0) for z in range(2)]
    rank = 4 * at_x + at_y
    late = [lax.dynamic_slice_in_dim(part, 24 * rank, 24, dim) for part, dim in ((w_qkv, 1), (w_out, 2), (w_up, 1), (w_down, 2))]
    late = [late[0].reshape(LAYERS, 24, 3 * BLOCK), late[1].transpose(0, 2, 1), late[2], late[3].transpose(0, 2, 1)]
    sooner = jnp.concatenate([late[2][0], late[3][0], late[0][1], late[1][1]], 1)
    later = jnp.concatenate([late[2][1], late[3][1]], 1)
    sooner = lax.all_gather(sooner, LINE + PLANE, axis=0, tiled=True).reshape(2, 2, HALF, -1)
    later = lax.all_gather(later, LINE + PLANE, axis=0, tiled=True).reshape(2, 2, HALF, -1)

    def part(late, z, start, count):
        return jnp.concatenate([late[0, z, :, start : start + count], late[1, z, :, start : start + count]], 0)

    weights_a = [first, [part(sooner, z, PACK_B, PACK_A) for z in range(2)]]
    weights_b = [[part(late, z, 0, PACK_B) for z in range(2)] for late in (sooner, later)]

    def both_blocks(value):
        other = swapped(value, "zl", 2, 1)
        pair = jnp.where(zl == 0, jnp.stack([value, other]), jnp.stack([other, value]))
        return jnp.concatenate([pair[0], pair[1]], -1)

    def both_halves(value):
        other = swapped(value, "row", 2, 1)
        pair = jnp.where(row == 0, jnp.stack([value, other]), jnp.stack([other, value]))
        return jnp.concatenate([pair[0], pair[1]], -1)

    column_small = both_blocks(jnp.concatenate([bias_qv.reshape(2, 2 * BLOCK), bias_up], 1)).astype(f32)
    column_small = column_small.reshape(LAYERS, 2, 2 * BLOCK + HID)
    feature_small = jnp.concatenate([bias_out[:, None], bias_down[:, None], ln_gain, ln_shift], 1)
    feature_small = both_halves(feature_small).astype(f32)

    mates = [(2 * z + 1, 4 + 2 * z) for z in range(2)] + [(4 + 2 * z, 2 * z + 1) for z in range(2)]
    everywhere = ("row", "zl", "core")
    at_home = core == row
    entered = jnp.concatenate([act_in, cotangent], 0)
    mine = jnp.where(at_home, entered, lax.ppermute(entered, everywhere, mates))
    other = swapped(mine, "core", 2, 1)
    entered = jnp.where(core == 0, jnp.concatenate([mine, other], 1), jnp.concatenate([other, mine], 1))
    length = lengths[0]
    ones = jnp.arange(QUARTER, dtype=jnp.int32)
    key_at = jnp.concatenate([(2 * (zl ^ (s & 1)) + (row ^ (s >> 1))) * QUARTER + ones for s in (0, 1, 3, 2)])
    key_ok = key_at < length
    own_ok = ((2 * zl + row) * QUARTER + ones < length)[:, None]

    kept = []
    state = entered[:QUARTER].astype(f32)
    for l in range(LAYERS):
        wa, wb = weights_a[l], weights_b[l]
        gain = feature_small[l, 2:4]
        shift = feature_small[l, 4:6]
        low = state.astype(bf16)
        qkv = []
        for z in range(2):
            value = mm(low, wa[z][:, : 3 * BLOCK])
            bias = column_small[l, z]
            bias = jnp.concatenate([bias[:BLOCK], jnp.zeros((BLOCK,), f32), bias[BLOCK : 2 * BLOCK]])
            qkv.append((value + bias).astype(bf16))
        query = jnp.concatenate([qkv[0][:, :BLOCK], qkv[1][:, :BLOCK]], 1)
        key_value = jnp.concatenate(
            [qkv[z][:, s * BLOCK : (s + 1) * BLOCK] for s in (1, 2) for z in range(2)], 1
        )
        key_value = jnp.concatenate(gather(key_value, LINE), 0)
        keys, values = key_value[:, : 2 * BLOCK], key_value[:, 2 * BLOCK :]
        mixture, probs = attend_forward(query, keys, values, key_ok)
        mixture = mixture.astype(bf16)
        branch = sum(mt(mixture[:, z * BLOCK : (z + 1) * BLOCK], wa[z][:, 3 * BLOCK :]) for z in range(2))
        branch = core_sum(branch) + feature_small[l, 0]
        normed, unit_one, inverse_one = norm_forward(state + branch, gain[0], shift[0])
        mix_parts = [mixture[:, z * BLOCK : (z + 1) * BLOCK] for z in range(2)]
        normed_low = normed.astype(bf16)
        pre = [mm(normed_low, wb[z][:, :HID]) + column_small[l, z, 2 * BLOCK :] for z in range(2)]
        hidden = [gelu_exact(pre[z]).astype(bf16) for z in range(2)]
        branch = sum(mt(hidden[z], wb[z][:, HID:]) for z in range(2))
        branch = core_sum(branch) + feature_small[l, 1]
        state, unit_two, inverse_two = norm_forward(normed + branch, gain[1], shift[1])
        kept.append(
            (low, mix_parts, query, keys, values, probs, unit_one, inverse_one, normed_low, pre, hidden, unit_two, inverse_two)
        )

    def to_output(value):
        halves = (value[:, :HALF], value[:, HALF:])
        sent = jnp.where(row == 0, halves[1], halves[0])
        here = jnp.where(row == 0, halves[0], halves[1])
        return jnp.where(at_home, here, lax.ppermute(sent, everywhere, mates))

    output = to_output(jnp.where(own_ok, state, 0.0).astype(bf16))
    grad_state = jnp.where(own_ok, entered[QUARTER:].astype(f32), 0.0)
    wide = []
    narrow = [[], []]
    for l in range(LAYERS - 1, -1, -1):
        low, mix_parts, query, keys, values, probs, unit_one, inverse_one, normed_low, pre, hidden, unit_two, inverse_two = kept[l]
        wa, wb = weights_a[l], weights_b[l]
        gain = feature_small[l, 2:4]
        resid_two, gain_two, shift_two = norm_backward(grad_state, unit_two, inverse_two, gain[1])
        grad_low = resid_two.astype(bf16)
        down_bias = jnp.sum(grad_low, 0, dtype=f32)
        pre_grad = []
        for z in range(2):
            hidden_grad = mm(grad_low, wb[z][:, HID:])
            pre_grad.append(jax.vjp(gelu_exact, pre[z])[1](hidden_grad)[0].astype(bf16))
        up_bias = [jnp.sum(pre_grad[z], 0, dtype=f32) for z in range(2)]
        normed_grad = resid_two + core_sum(sum(mt(pre_grad[z], wb[z][:, :HID]) for z in range(2)))
        pieces = plane_pieces(weight_grad([(normed_low, pre_grad), (grad_low, hidden)]))
        if l == 1:
            one = plane_exchange(pieces)
        else:
            one = line_sum(one.reshape(4, 96, HALF).astype(bf16), place).astype(bf16)
            zero = plane_exchange(jnp.concatenate([pieces, one_a.astype(bf16).reshape(16, 48, HALF)], 1))
        resid_one, gain_one, shift_one = norm_backward(normed_grad, unit_one, inverse_one, gain[0])
        attn_low = resid_one.astype(bf16)
        out_bias = jnp.sum(attn_low, 0, dtype=f32)
        mixture_grad = jnp.concatenate([mm(attn_low, wa[z][:, 3 * BLOCK :]) for z in range(2)], 1).astype(bf16)
        query_grad, key_grad, value_grad = attend_backward(query, keys, values, probs, mixture_grad)
        key_value_grad = jnp.concatenate([key_grad, value_grad], 1).reshape(4, QUARTER, 4 * BLOCK)
        parts = [swapped(key_value_grad[i].astype(bf16), LINE, 4, bits) for i, bits in ((1, 1), (2, 3), (3, 2))]
        key_value_grad = key_value_grad[0] + sum(part.astype(f32) for part in parts)
        if l == 0:
            key_value_grad = key_value_grad + when(one)
            one = lax.all_gather(one, PLANE, axis=0, tiled=True)
        qkv_grad = []
        for z in range(2):
            cut = slice(z * BLOCK, (z + 1) * BLOCK)
            later = slice((z + 2) * BLOCK, (z + 3) * BLOCK)
            qkv_grad.append(
                jnp.concatenate([query_grad[:, cut], key_value_grad[:, cut], key_value_grad[:, later]], 1).astype(bf16)
            )
        qkv_bias = [jnp.sum(qkv_grad[z], 0, dtype=f32) for z in range(2)]
        grad_state = resid_one + core_sum(sum(mt(qkv_grad[z], wa[z][:, : 3 * BLOCK]) for z in range(2)))
        full_a = weight_grad([(low, qkv_grad), (attn_low, mix_parts)])
        if l == 1:
            one = plane_sum(one)
            grad_state = grad_state + when(one)
            one_a = line_sum(full_a.reshape(4, PACK_A, HALF), place)
        else:
            zero_a = line_sum(full_a.reshape(4, PACK_A, HALF), place)
            zero = plane_sum(zero) + when(one)
        wide += [out_bias, down_bias, gain_one, gain_two, shift_one, shift_two]
        narrow = [narrow[z] + [qkv_bias[z], up_bias[z]] for z in range(2)]

    grad_in = to_output(grad_state)

    wide = jnp.stack(wide)
    narrow = [jnp.concatenate(part) for part in narrow]
    small = jnp.stack(
        [jnp.concatenate([wide[:, (j // 2) * HALF : (j // 2 + 1) * HALF].reshape(-1), narrow[j % 2]]) for j in range(4)]
    )
    small = split3(jnp.pad(line_sum(small.reshape(4, SMALL, HALF), place), ((0, 32 - SMALL), (0, 0))))
    small = small.reshape(3, 16, 2, HALF).transpose(1, 0, 2, 3).reshape(16, 6, HALF)
    zero_a = (zero_a + when(zero)).astype(bf16).reshape(16, 48, HALF)
    moved = plane_exchange(jnp.concatenate([zero_a, small, jnp.zeros((16, 2, HALF), bf16)], 1))
    zero_b = line_sum(zero[:HALF].reshape(4, 96, HALF).astype(bf16), place).astype(bf16)
    small = split3(jnp.sum(moved[:, 48:54].reshape(48, 2, HALF), 0, dtype=f32)).reshape(6, HALF)
    zero_a = plane_sum(moved[:, :48]).astype(bf16)
    zero = jnp.concatenate([zero_b, zero[HALF:].astype(bf16), zero_a, small, jnp.zeros((2, HALF), bf16)], 0)
    zero = jnp.stack(in_order(near_first(gather(zero, "y")), at_y))
    zero = jnp.stack(in_order(near_first(gather(zero, "x")), at_x)).reshape(16, 200, HALF)
    own = jnp.sum(zero[:, 192:198].reshape(16, 3, 2, HALF), 1, dtype=f32).reshape(32 * HALF)
    wide = own[: 12 * HALF].reshape(LAYERS, 6, HALF)[::-1]
    own = own[12 * HALF : SMALL * HALF].reshape(LAYERS, 3 * BLOCK + HID)[::-1]
    grad_a = [zero[:, 144:192].reshape(PACK_A, HALF), zero[:, 96:144].reshape(PACK_A, HALF)]
    grad_b = [zero[:, :96].reshape(PACK_B, HALF), one.reshape(PACK_B, HALF)]

    def both(parts, turn):
        return jnp.stack([part.T if turn else part for part in parts]).astype(f32)

    return (
        output,
        grad_in,
        both([part[: 3 * BLOCK] for part in grad_a], True).reshape(LAYERS, HALF, 3, BLOCK),
        jnp.stack([own[:, :BLOCK], own[:, 2 * BLOCK : 3 * BLOCK]], 1),
        both([part[3 * BLOCK :] for part in grad_a], False),
        wide[:, 0],
        both([part[:HID] for part in grad_b], True),
        own[:, 3 * BLOCK :],
        both([part[HID:] for part in grad_b], False),
        wide[:, 1],
        wide[:, 2:4],
        wide[:, 4:6],
    )


def solution(mesh):
    fine = Mesh(mesh.devices.reshape(4, 4, 2, 2, 2), ("x", "y", "row", "zl", "core"))
    tokens = P(("x", "y", "zl", "core"), "row")
    col = ("zl", "core")
    in_specs = (
        tokens,
        tokens,
        P(("x", "y")),
        P(None, "row", None, col),
        P(None, None, col),
        P(None, col, "row"),
        P(None, "row"),
        P(None, "row", col),
        P(None, col),
        P(None, col, "row"),
        P(None, "row"),
        P(None, None, "row"),
        P(None, None, "row"),
    )
    out_specs = (tokens, tokens) + in_specs[3:8] + (in_specs[8],) + in_specs[9:11] + (in_specs[11], in_specs[12])
    return jax.shard_map(on_device, mesh=fine, in_specs=in_specs, out_specs=out_specs, check_vma=False)
```

```python
import jax
import jax.numpy as jnp
from jax import lax
from jax.sharding import Mesh
from jax.sharding import PartitionSpec as P

LAYERS = 2
HDIM = 64
HEADS = 6
GROUP = 1024
QUARTER = 256
WIDTH = 768
HALF = 384
BLOCK = 192
HID = 768
PACK_A = 768
PACK_B = 1536
SMALL = 19

EPSILON = 1e-05
MASKED = -1000000000.0

LINE = ("row", "zl")
PLANE = ("x", "y")
bf16 = jnp.bfloat16
f32 = jnp.float32


def swapped(value, axes, count, bits):
    return lax.ppermute(value, axes, [(i, i ^ bits) for i in range(count)])


def in_order(parts, place):
    flip = (place % 2) == 1
    parts = [jnp.where(flip, parts[s ^ 1], parts[s]) for s in range(4)]
    flip = (place // 2) == 1
    return [jnp.where(flip, parts[s ^ 2], parts[s]) for s in range(4)]


def gather(value, axes):
    return [value] + [swapped(value, axes, 4, bits) for bits in (1, 3, 2)]


def near_first(parts):
    return [parts[0], parts[1], parts[3], parts[2]]


def piece_of(value, index, dim):
    return lax.dynamic_index_in_dim(value, index, dim, keepdims=False)


def split3(value):
    high = lax.reduce_precision(value, 8, 7)
    rest = value - high
    middle = lax.reduce_precision(rest, 8, 7)
    return jnp.stack([high, middle, rest - middle]).astype(bf16)


def dot(left, right, dims):
    return lax.dot_general(left, right, ((dims[0], dims[1]), ((), ())), preferred_element_type=f32)


def mm(left, right):
    return dot(left, right, ((1,), (0,)))


def mt(left, right):
    return dot(left, right, ((1,), (1,)))


def tm(left, right):
    return dot(left, right, ((0,), (0,)))


def core_sum(value):
    return value + swapped(value, "core", 2, 1)


def norm_forward(resid, gain, shift):
    mean = jnp.mean(resid, 1, keepdims=True)
    square = jnp.mean(resid * resid, 1, keepdims=True)
    inverse = lax.rsqrt(square - mean * mean + EPSILON)
    unit = (resid - mean) * inverse
    return unit * gain + shift, unit, inverse


def norm_backward(grad, unit, inverse, gain):
    scaled = grad * gain
    first = jnp.mean(scaled, 1, keepdims=True)
    second = jnp.mean(scaled * unit, 1, keepdims=True)
    resid_grad = inverse * (scaled - first - unit * second)
    return resid_grad, jnp.sum(grad * unit, 0), jnp.sum(grad, 0)


def heads_of(value):
    return value.reshape(value.shape[0], HEADS, HDIM)


def attend_forward(query, keys, values, key_ok):
    scores = jnp.einsum("qhd,khd->hqk", heads_of(query), heads_of(keys), preferred_element_type=f32) * 0.125
    scores = jnp.where(key_ok[None, None, :], scores, MASKED)
    peak = jnp.max(scores, axis=2, keepdims=True)
    raised = jnp.exp(scores - peak)
    probs = raised / jnp.sum(raised, axis=2, keepdims=True)
    mixture = jnp.einsum("hqk,khd->qhd", probs.astype(bf16), heads_of(values), preferred_element_type=f32)
    return mixture.reshape(QUARTER, HEADS * HDIM), probs


def attend_backward(query, keys, values, probs, grad):
    grad = heads_of(grad)
    grad_probs = jnp.einsum("qhd,khd->hqk", grad, heads_of(values), preferred_element_type=f32)
    inner = jnp.sum(probs * grad_probs, axis=2, keepdims=True)
    grad_scores = (probs * (grad_probs - inner)).astype(bf16)
    query_grad = jnp.einsum("hqk,khd->qhd", grad_scores, heads_of(keys), preferred_element_type=f32) * 0.125
    key_grad = jnp.einsum("hqk,qhd->khd", grad_scores, heads_of(query), preferred_element_type=f32) * 0.125
    value_grad = jnp.einsum("hqk,qhd->khd", probs.astype(bf16), grad, preferred_element_type=f32)
    return (
        query_grad.reshape(QUARTER, HEADS * HDIM),
        key_grad.reshape(GROUP, HEADS * HDIM),
        value_grad.reshape(GROUP, HEADS * HDIM),
    )


def gelu_exact(value):
    return jax.nn.gelu(value, approximate=False)


def weight_grad(pairs, extra=None):
    blocks = []
    for row in range(2):
        for z in range(2):
            blocks += [tm(right[z], left[:, row * HALF : (row + 1) * HALF]).astype(bf16) for left, right in pairs]
            if extra is not None:
                blocks.append(extra[2 * row + z])
    return jnp.concatenate(blocks, 0)


def plane_pieces(pieces):
    return pieces.reshape(4, 16, -1, HALF).transpose(1, 0, 2, 3).reshape(16, -1, HALF)


def plane_exchange(pieces):
    return lax.all_to_all(pieces, PLANE, 0, 0, tiled=True)


def plane_sum(received):
    return jnp.sum(received, 0, dtype=f32)


def line_sum(pieces, place):
    total = piece_of(pieces, place, 0).astype(f32)
    for bits in (1, 3, 2):
        total = total + swapped(piece_of(pieces, place ^ bits, 0), LINE, 4, bits).astype(f32)
    return total


def when(value):
    return lax.slice(value, (0,) * value.ndim, (1,) * value.ndim).reshape(()).astype(f32) * 0.0


def on_device(
    act_in, cotangent, lengths, w_qkv, bias_qv, w_out, bias_out, w_up, bias_up, w_down, bias_down, ln_gain, ln_shift
):
    at_x, at_y = lax.axis_index("x"), lax.axis_index("y")
    row, zl, core = lax.axis_index("row"), lax.axis_index("zl"), lax.axis_index("core")
    place = 2 * row + zl

    first = in_order(near_first(gather(jnp.concatenate([w_qkv[0].reshape(HALF, 3 * BLOCK), w_out[0].T], 1), LINE)), place)
    first = [jnp.concatenate([first[z], first[2 + z]], 0) for z in range(2)]
    rank = 4 * at_x + at_y
    late = [lax.dynamic_slice_in_dim(part, 24 * rank, 24, dim) for part, dim in ((w_qkv, 1), (w_out, 2), (w_up, 1), (w_down, 2))]
    late = [late[0].reshape(LAYERS, 24, 3 * BLOCK), late[1].transpose(0, 2, 1), late[2], late[3].transpose(0, 2, 1)]
    sooner = jnp.concatenate([late[2][0], late[3][0], late[0][1], late[1][1]], 1)
    later = jnp.concatenate([late[2][1], late[3][1]], 1)
    sooner = lax.all_gather(sooner, LINE + PLANE, axis=0, tiled=True).reshape(2, 2, HALF, -1)
    later = lax.all_gather(later, LINE + PLANE, axis=0, tiled=True).reshape(2, 2, HALF, -1)

    def part(late, z, start, count):
        return jnp.concatenate([late[0, z, :, start : start + count], late[1, z, :, start : start + count]], 0)

    weights_a = [first, [part(sooner, z, PACK_B, PACK_A) for z in range(2)]]
    weights_b = [[part(late, z, 0, PACK_B) for z in range(2)] for late in (sooner, later)]

    def both_blocks(value):
        other = swapped(value, "zl", 2, 1)
        pair = jnp.where(zl == 0, jnp.stack([value, other]), jnp.stack([other, value]))
        return jnp.concatenate([pair[0], pair[1]], -1)

    def both_halves(value):
        other = swapped(value, "row", 2, 1)
        pair = jnp.where(row == 0, jnp.stack([value, other]), jnp.stack([other, value]))
        return jnp.concatenate([pair[0], pair[1]], -1)

    column_small = both_blocks(jnp.concatenate([bias_qv.reshape(2, 2 * BLOCK), bias_up], 1)).astype(f32)
    column_small = column_small.reshape(LAYERS, 2, 2 * BLOCK + HID)
    feature_small = jnp.concatenate([bias_out[:, None], bias_down[:, None], ln_gain, ln_shift], 1)
    feature_small = both_halves(feature_small).astype(f32)

    mates = [(2 * z + 1, 4 + 2 * z) for z in range(2)] + [(4 + 2 * z, 2 * z + 1) for z in range(2)]
    everywhere = ("row", "zl", "core")
    at_home = core == row
    entered = jnp.concatenate([act_in, cotangent], 0)
    mine = jnp.where(at_home, entered, lax.ppermute(entered, everywhere, mates))
    other = swapped(mine, "core", 2, 1)
    entered = jnp.where(core == 0, jnp.concatenate([mine, other], 1), jnp.concatenate([other, mine], 1))
    length = lengths[0]
    ones = jnp.arange(QUARTER, dtype=jnp.int32)
    key_at = jnp.concatenate([(2 * (zl ^ (s & 1)) + (row ^ (s >> 1))) * QUARTER + ones for s in (0, 1, 3, 2)])
    key_ok = key_at < length
    own_ok = ((2 * zl + row) * QUARTER + ones < length)[:, None]

    kept = []
    state = entered[:QUARTER].astype(f32)
    for l in range(LAYERS):
        wa, wb = weights_a[l], weights_b[l]
        gain = feature_small[l, 2:4]
        shift = feature_small[l, 4:6]
        low = state.astype(bf16)
        qkv = []
        for z in range(2):
            value = mm(low, wa[z][:, : 3 * BLOCK])
            bias = column_small[l, z]
            bias = jnp.concatenate([bias[:BLOCK], jnp.zeros((BLOCK,), f32), bias[BLOCK : 2 * BLOCK]])
            qkv.append((value + bias).astype(bf16))
        query = jnp.concatenate([qkv[0][:, :BLOCK], qkv[1][:, :BLOCK]], 1)
        key_value = jnp.concatenate(
            [qkv[z][:, s * BLOCK : (s + 1) * BLOCK] for s in (1, 2) for z in range(2)], 1
        )
        key_value = jnp.concatenate(gather(key_value, LINE), 0)
        keys, values = key_value[:, : 2 * BLOCK], key_value[:, 2 * BLOCK :]
        mixture, probs = attend_forward(query, keys, values, key_ok)
        mixture = mixture.astype(bf16)
        branch = sum(mt(mixture[:, z * BLOCK : (z + 1) * BLOCK], wa[z][:, 3 * BLOCK :]) for z in range(2))
        branch = core_sum(branch) + feature_small[l, 0]
        normed, unit_one, inverse_one = norm_forward(state + branch, gain[0], shift[0])
        mix_parts = [mixture[:, z * BLOCK : (z + 1) * BLOCK] for z in range(2)]
        normed_low = normed.astype(bf16)
        pre = [mm(normed_low, wb[z][:, :HID]) + column_small[l, z, 2 * BLOCK :] for z in range(2)]
        hidden = [gelu_exact(pre[z]).astype(bf16) for z in range(2)]
        branch = sum(mt(hidden[z], wb[z][:, HID:]) for z in range(2))
        branch = core_sum(branch) + feature_small[l, 1]
        state, unit_two, inverse_two = norm_forward(normed + branch, gain[1], shift[1])
        kept.append(
            (low, mix_parts, query, keys, values, probs, unit_one, inverse_one, normed_low, pre, hidden, unit_two, inverse_two)
        )

    def to_output(value):
        halves = (value[:, :HALF], value[:, HALF:])
        sent = jnp.where(row == 0, halves[1], halves[0])
        here = jnp.where(row == 0, halves[0], halves[1])
        return jnp.where(at_home, here, lax.ppermute(sent, everywhere, mates))

    output = to_output(jnp.where(own_ok, state, 0.0).astype(bf16))
    grad_state = jnp.where(own_ok, entered[QUARTER:].astype(f32), 0.0)
    wide = []
    narrow = [[], []]
    for l in range(LAYERS - 1, -1, -1):
        low, mix_parts, query, keys, values, probs, unit_one, inverse_one, normed_low, pre, hidden, unit_two, inverse_two = kept[l]
        wa, wb = weights_a[l], weights_b[l]
        gain = feature_small[l, 2:4]
        resid_two, gain_two, shift_two = norm_backward(grad_state, unit_two, inverse_two, gain[1])
        grad_low = resid_two.astype(bf16)
        down_bias = jnp.sum(grad_low, 0, dtype=f32)
        pre_grad = []
        for z in range(2):
            hidden_grad = mm(grad_low, wb[z][:, HID:])
            pre_grad.append(jax.vjp(gelu_exact, pre[z])[1](hidden_grad)[0].astype(bf16))
        up_bias = [jnp.sum(pre_grad[z], 0, dtype=f32) for z in range(2)]
        normed_grad = resid_two + core_sum(sum(mt(pre_grad[z], wb[z][:, :HID]) for z in range(2)))
        pieces = plane_pieces(weight_grad([(normed_low, pre_grad), (grad_low, hidden)]))
        if l == 1:
            one = plane_exchange(pieces)
        else:
            one = line_sum(one.reshape(4, 96, HALF).astype(bf16), place).astype(bf16)
            one = jnp.concatenate([one, plane_sum(one_a).astype(bf16)], 0)
            zero = plane_exchange(pieces)
        resid_one, gain_one, shift_one = norm_backward(normed_grad, unit_one, inverse_one, gain[0])
        attn_low = resid_one.astype(bf16)
        out_bias = jnp.sum(attn_low, 0, dtype=f32)
        mixture_grad = jnp.concatenate([mm(attn_low, wa[z][:, 3 * BLOCK :]) for z in range(2)], 1).astype(bf16)
        query_grad, key_grad, value_grad = attend_backward(query, keys, values, probs, mixture_grad)
        key_value_grad = jnp.concatenate([key_grad, value_grad], 1).reshape(4, QUARTER, 4 * BLOCK)
        parts = [swapped(key_value_grad[i].astype(bf16), LINE, 4, bits) for i, bits in ((1, 1), (2, 3), (3, 2))]
        key_value_grad = key_value_grad[0] + sum(part.astype(f32) for part in parts)
        if l == 0:
            key_value_grad = key_value_grad + when(one)
            one = lax.all_gather(one, PLANE, axis=0, tiled=True)
        qkv_grad = []
        for z in range(2):
            cut = slice(z * BLOCK, (z + 1) * BLOCK)
            later = slice((z + 2) * BLOCK, (z + 3) * BLOCK)
            qkv_grad.append(
                jnp.concatenate([query_grad[:, cut], key_value_grad[:, cut], key_value_grad[:, later]], 1).astype(bf16)
            )
        qkv_bias = [jnp.sum(qkv_grad[z], 0, dtype=f32) for z in range(2)]
        grad_state = resid_one + core_sum(sum(mt(qkv_grad[z], wa[z][:, : 3 * BLOCK]) for z in range(2)))
        wide = [out_bias, down_bias, gain_one, gain_two, shift_one, shift_two] + wide
        narrow = [[qkv_bias[z], up_bias[z]] + narrow[z] for z in range(2)]
        pairs_a = [(low, qkv_grad), (attn_low, mix_parts)]
        if l == 1:
            one = plane_sum(one)
            grad_state = grad_state + when(one)
            one_a = (line_sum(weight_grad(pairs_a).reshape(4, PACK_A, HALF), place) + when(one)).astype(bf16)
            one_a = plane_exchange(one_a.reshape(16, 48, HALF))
        else:
            wide = jnp.stack(wide)
            small = [
                jnp.concatenate([wide[:, (j // 2) * HALF : (j // 2 + 1) * HALF].reshape(-1)] + narrow[j % 2])
                for j in range(4)
            ]
            small = split3(jnp.stack(small).reshape(4, SMALL, HALF)).transpose(1, 0, 2, 3).reshape(4, 3 * SMALL, HALF)
            small = jnp.pad(small, ((0, 0), (0, 64 - 3 * SMALL), (0, 0)))
            zero_a = line_sum(weight_grad(pairs_a, small).reshape(4, PACK_A + 64, HALF), place)
            zero = plane_sum(zero) + when(one)

    grad_in = to_output(grad_state)

    small = jnp.sum(zero_a[PACK_A : PACK_A + 3 * SMALL].reshape(3, SMALL, HALF), 0)
    small = split3(jnp.pad(small, ((0, 32 - SMALL), (0, 0))))
    small = small.reshape(3, 16, 2, HALF).transpose(1, 0, 2, 3).reshape(16, 6, HALF)
    zero_a = (zero_a[:PACK_A] + when(zero)).astype(bf16).reshape(16, 48, HALF)
    moved = plane_exchange(jnp.concatenate([zero_a, small, jnp.zeros((16, 2, HALF), bf16)], 1))
    zero_b = line_sum(zero.reshape(4, 96, HALF).astype(bf16), place).astype(bf16)
    small = split3(jnp.sum(moved[:, 48:54].reshape(48, 2, HALF), 0, dtype=f32)).reshape(6, HALF)
    zero_a = plane_sum(moved[:, :48]).astype(bf16)
    zero = jnp.concatenate([zero_b, zero_a, small, jnp.zeros((2, HALF), bf16)], 0)
    zero = jnp.stack(in_order(near_first(gather(zero, "y")), at_y))
    zero = jnp.stack(in_order(near_first(gather(zero, "x")), at_x)).reshape(16, 152, HALF)
    own = jnp.sum(zero[:, 144:150].reshape(16, 3, 2, HALF), 1, dtype=f32).reshape(32 * HALF)
    wide = own[: 12 * HALF].reshape(LAYERS, 6, HALF)
    own = own[12 * HALF : SMALL * HALF].reshape(LAYERS, 3 * BLOCK + HID)
    one = one.reshape(16, 144, HALF)
    grad_a = [zero[:, 96:144].reshape(PACK_A, HALF), one[:, 96:].reshape(PACK_A, HALF)]
    grad_b = [zero[:, :96].reshape(PACK_B, HALF), one[:, :96].reshape(PACK_B, HALF)]

    def both(parts, turn):
        return jnp.stack([part.T if turn else part for part in parts]).astype(f32)

    return (
        output,
        grad_in,
        both([part[: 3 * BLOCK] for part in grad_a], True).reshape(LAYERS, HALF, 3, BLOCK),
        jnp.stack([own[:, :BLOCK], own[:, 2 * BLOCK : 3 * BLOCK]], 1),
        both([part[3 * BLOCK :] for part in grad_a], False),
        wide[:, 0],
        both([part[:HID] for part in grad_b], True),
        own[:, 3 * BLOCK :],
        both([part[HID:] for part in grad_b], False),
        wide[:, 1],
        wide[:, 2:4],
        wide[:, 4:6],
    )


def solution(mesh):
    fine = Mesh(mesh.devices.reshape(4, 4, 2, 2, 2), ("x", "y", "row", "zl", "core"))
    tokens = P(("x", "y", "zl", "core"), "row")
    col = ("zl", "core")
    in_specs = (
        tokens,
        tokens,
        P(("x", "y")),
        P(None, "row", None, col),
        P(None, None, col),
        P(None, col, "row"),
        P(None, "row"),
        P(None, "row", col),
        P(None, col),
        P(None, col, "row"),
        P(None, "row"),
        P(None, None, "row"),
        P(None, None, "row"),
    )
    out_specs = (tokens, tokens) + in_specs[3:8] + (in_specs[8],) + in_specs[9:11] + (in_specs[11], in_specs[12])
    return jax.shard_map(on_device, mesh=fine, in_specs=in_specs, out_specs=out_specs, check_vma=False)
```

```python
import jax
import jax.numpy as jnp
from jax import lax
from jax.sharding import Mesh
from jax.sharding import PartitionSpec as P

LAYERS = 2
HDIM = 64
HEADS = 6
GROUP = 1024
QUARTER = 256
WIDTH = 768
HALF = 384
BLOCK = 192
HID = 768
PACK_A = 768
PACK_B = 1536
SMALL = 19

EPSILON = 1e-05
MASKED = -1000000000.0

LINE = ("row", "zl")
PLANE = ("x", "y")
bf16 = jnp.bfloat16
f32 = jnp.float32


def swapped(value, axes, count, bits):
    return lax.ppermute(value, axes, [(i, i ^ bits) for i in range(count)])


def in_order(parts, place):
    flip = (place % 2) == 1
    parts = [jnp.where(flip, parts[s ^ 1], parts[s]) for s in range(4)]
    flip = (place // 2) == 1
    return [jnp.where(flip, parts[s ^ 2], parts[s]) for s in range(4)]


def gather(value, axes):
    return [value] + [swapped(value, axes, 4, bits) for bits in (1, 3, 2)]


def near_first(parts):
    return [parts[0], parts[1], parts[3], parts[2]]


def piece_of(value, index, dim):
    return lax.dynamic_index_in_dim(value, index, dim, keepdims=False)


def split3(value):
    high = lax.reduce_precision(value, 8, 7)
    rest = value - high
    middle = lax.reduce_precision(rest, 8, 7)
    return jnp.stack([high, middle, rest - middle]).astype(bf16)


def dot(left, right, dims):
    return lax.dot_general(left, right, ((dims[0], dims[1]), ((), ())), preferred_element_type=f32)


def mm(left, right):
    return dot(left, right, ((1,), (0,)))


def mt(left, right):
    return dot(left, right, ((1,), (1,)))


def tm(left, right):
    return dot(left, right, ((0,), (0,)))


def core_sum(value):
    return value + swapped(value, "core", 2, 1)


def norm_forward(resid, gain, shift):
    mean = jnp.mean(resid, 1, keepdims=True)
    square = jnp.mean(resid * resid, 1, keepdims=True)
    inverse = lax.rsqrt(square - mean * mean + EPSILON)
    unit = (resid - mean) * inverse
    return unit * gain + shift, unit, inverse


def norm_backward(grad, unit, inverse, gain):
    scaled = grad * gain
    first = jnp.mean(scaled, 1, keepdims=True)
    second = jnp.mean(scaled * unit, 1, keepdims=True)
    resid_grad = inverse * (scaled - first - unit * second)
    return resid_grad, jnp.sum(grad * unit, 0), jnp.sum(grad, 0)


def heads_of(value):
    return value.reshape(value.shape[0], HEADS, HDIM)


def attend_forward(query, keys, values, key_ok):
    scores = jnp.einsum("qhd,khd->hqk", heads_of(query), heads_of(keys), preferred_element_type=f32) * 0.125
    scores = jnp.where(key_ok[None, None, :], scores, MASKED)
    peak = jnp.max(scores, axis=2, keepdims=True)
    raised = jnp.exp(scores - peak)
    probs = raised / jnp.sum(raised, axis=2, keepdims=True)
    mixture = jnp.einsum("hqk,khd->qhd", probs.astype(bf16), heads_of(values), preferred_element_type=f32)
    return mixture.reshape(QUARTER, HEADS * HDIM), probs


def attend_backward(query, keys, values, probs, grad):
    grad = heads_of(grad)
    grad_probs = jnp.einsum("qhd,khd->hqk", grad, heads_of(values), preferred_element_type=f32)
    inner = jnp.sum(probs * grad_probs, axis=2, keepdims=True)
    grad_scores = (probs * (grad_probs - inner)).astype(bf16)
    query_grad = jnp.einsum("hqk,khd->qhd", grad_scores, heads_of(keys), preferred_element_type=f32) * 0.125
    key_grad = jnp.einsum("hqk,qhd->khd", grad_scores, heads_of(query), preferred_element_type=f32) * 0.125
    value_grad = jnp.einsum("hqk,qhd->khd", probs.astype(bf16), grad, preferred_element_type=f32)
    return (
        query_grad.reshape(QUARTER, HEADS * HDIM),
        key_grad.reshape(GROUP, HEADS * HDIM),
        value_grad.reshape(GROUP, HEADS * HDIM),
    )


def gelu_exact(value):
    return jax.nn.gelu(value, approximate=False)


def weight_grad(pairs, extra=None):
    blocks = []
    for row in range(2):
        for z in range(2):
            blocks += [tm(right[z], left[:, row * HALF : (row + 1) * HALF]).astype(bf16) for left, right in pairs]
            if extra is not None:
                blocks.append(extra[2 * row + z])
    return jnp.concatenate(blocks, 0)


def plane_pieces(pieces):
    return pieces.reshape(4, 16, -1, HALF).transpose(1, 0, 2, 3).reshape(16, -1, HALF)


def plane_exchange(pieces):
    return lax.all_to_all(pieces, PLANE, 0, 0, tiled=True)


def plane_sum(received):
    return jnp.sum(received, 0, dtype=f32)


def line_sum(pieces, place):
    total = piece_of(pieces, place, 0).astype(f32)
    for bits in (1, 3, 2):
        total = total + swapped(piece_of(pieces, place ^ bits, 0), LINE, 4, bits).astype(f32)
    return total


def when(value):
    return lax.slice(value, (0,) * value.ndim, (1,) * value.ndim).reshape(()).astype(f32) * 0.0


def on_device(
    act_in, cotangent, lengths, w_qkv, bias_qv, w_out, bias_out, w_up, bias_up, w_down, bias_down, ln_gain, ln_shift
):
    at_x, at_y = lax.axis_index("x"), lax.axis_index("y")
    row, zl, core = lax.axis_index("row"), lax.axis_index("zl"), lax.axis_index("core")
    place = 2 * row + zl

    first = in_order(near_first(gather(jnp.concatenate([w_qkv[0].reshape(HALF, 3 * BLOCK), w_out[0].T], 1), LINE)), place)
    first = [jnp.concatenate([first[z], first[2 + z]], 0) for z in range(2)]
    rank = 4 * at_x + at_y
    late = [lax.dynamic_slice_in_dim(part, 24 * rank, 24, dim) for part, dim in ((w_qkv, 1), (w_out, 2), (w_up, 1), (w_down, 2))]
    late = [late[0].reshape(LAYERS, 24, 3 * BLOCK), late[1].transpose(0, 2, 1), late[2], late[3].transpose(0, 2, 1)]
    sooner = jnp.concatenate([late[2][0], late[3][0], late[0][1], late[1][1]], 1)
    later = jnp.concatenate([late[2][1], late[3][1]], 1)
    sooner = lax.all_gather(sooner, LINE + PLANE, axis=0, tiled=True).reshape(2, 2, HALF, -1)
    later = lax.all_gather(later, LINE + PLANE, axis=0, tiled=True).reshape(2, 2, HALF, -1)

    def part(late, z, start, count):
        return jnp.concatenate([late[0, z, :, start : start + count], late[1, z, :, start : start + count]], 0)

    weights_a = [first, [part(sooner, z, PACK_B, PACK_A) for z in range(2)]]
    weights_b = [[part(late, z, 0, PACK_B) for z in range(2)] for late in (sooner, later)]

    def both_blocks(value):
        other = swapped(value, "zl", 2, 1)
        pair = jnp.where(zl == 0, jnp.stack([value, other]), jnp.stack([other, value]))
        return jnp.concatenate([pair[0], pair[1]], -1)

    def both_halves(value):
        other = swapped(value, "row", 2, 1)
        pair = jnp.where(row == 0, jnp.stack([value, other]), jnp.stack([other, value]))
        return jnp.concatenate([pair[0], pair[1]], -1)

    column_small = both_blocks(jnp.concatenate([bias_qv.reshape(2, 2 * BLOCK), bias_up], 1)).astype(f32)
    column_small = column_small.reshape(LAYERS, 2, 2 * BLOCK + HID)
    feature_small = jnp.concatenate([bias_out[:, None], bias_down[:, None], ln_gain, ln_shift], 1)
    feature_small = both_halves(feature_small).astype(f32)

    mates = [(2 * z + 1, 4 + 2 * z) for z in range(2)] + [(4 + 2 * z, 2 * z + 1) for z in range(2)]
    everywhere = ("row", "zl", "core")
    at_home = core == row
    entered = jnp.concatenate([act_in, cotangent], 0)
    mine = jnp.where(at_home, entered, lax.ppermute(entered, everywhere, mates))
    other = swapped(mine, "core", 2, 1)
    entered = jnp.where(core == 0, jnp.concatenate([mine, other], 1), jnp.concatenate([other, mine], 1))
    length = lengths[0]
    ones = jnp.arange(QUARTER, dtype=jnp.int32)
    key_at = jnp.concatenate([(2 * (zl ^ (s & 1)) + (row ^ (s >> 1))) * QUARTER + ones for s in (0, 1, 3, 2)])
    key_ok = key_at < length
    own_ok = ((2 * zl + row) * QUARTER + ones < length)[:, None]

    kept = []
    state = entered[:QUARTER].astype(f32)
    for l in range(LAYERS):
        wa, wb = weights_a[l], weights_b[l]
        gain = feature_small[l, 2:4]
        shift = feature_small[l, 4:6]
        low = state.astype(bf16)
        qkv = []
        for z in range(2):
            value = mm(low, wa[z][:, : 3 * BLOCK])
            bias = column_small[l, z]
            bias = jnp.concatenate([bias[:BLOCK], jnp.zeros((BLOCK,), f32), bias[BLOCK : 2 * BLOCK]])
            qkv.append((value + bias).astype(bf16))
        query = jnp.concatenate([qkv[0][:, :BLOCK], qkv[1][:, :BLOCK]], 1)
        key_value = jnp.concatenate(
            [qkv[z][:, s * BLOCK : (s + 1) * BLOCK] for s in (1, 2) for z in range(2)], 1
        )
        key_value = jnp.concatenate(gather(key_value, LINE), 0)
        keys, values = key_value[:, : 2 * BLOCK], key_value[:, 2 * BLOCK :]
        mixture, probs = attend_forward(query, keys, values, key_ok)
        mixture = mixture.astype(bf16)
        branch = sum(mt(mixture[:, z * BLOCK : (z + 1) * BLOCK], wa[z][:, 3 * BLOCK :]) for z in range(2))
        branch = core_sum(branch) + feature_small[l, 0]
        normed, unit_one, inverse_one = norm_forward(state + branch, gain[0], shift[0])
        mix_parts = [mixture[:, z * BLOCK : (z + 1) * BLOCK] for z in range(2)]
        normed_low = normed.astype(bf16)
        pre = [mm(normed_low, wb[z][:, :HID]) + column_small[l, z, 2 * BLOCK :] for z in range(2)]
        hidden = [gelu_exact(pre[z]).astype(bf16) for z in range(2)]
        branch = sum(mt(hidden[z], wb[z][:, HID:]) for z in range(2))
        branch = core_sum(branch) + feature_small[l, 1]
        state, unit_two, inverse_two = norm_forward(normed + branch, gain[1], shift[1])
        kept.append(
            (low, mix_parts, query, keys, values, probs, unit_one, inverse_one, normed_low, pre, hidden, unit_two, inverse_two)
        )

    def to_output(value):
        halves = (value[:, :HALF], value[:, HALF:])
        sent = jnp.where(row == 0, halves[1], halves[0])
        here = jnp.where(row == 0, halves[0], halves[1])
        return jnp.where(at_home, here, lax.ppermute(sent, everywhere, mates))

    output = to_output(jnp.where(own_ok, state, 0.0).astype(bf16))
    grad_state = jnp.where(own_ok, entered[QUARTER:].astype(f32), 0.0)
    wide = []
    narrow = [[], []]
    for l in range(LAYERS - 1, -1, -1):
        low, mix_parts, query, keys, values, probs, unit_one, inverse_one, normed_low, pre, hidden, unit_two, inverse_two = kept[l]
        wa, wb = weights_a[l], weights_b[l]
        gain = feature_small[l, 2:4]
        resid_two, gain_two, shift_two = norm_backward(grad_state, unit_two, inverse_two, gain[1])
        grad_low = resid_two.astype(bf16)
        down_bias = jnp.sum(grad_low, 0, dtype=f32)
        pre_grad = []
        for z in range(2):
            hidden_grad = mm(grad_low, wb[z][:, HID:])
            pre_grad.append(jax.vjp(gelu_exact, pre[z])[1](hidden_grad)[0].astype(bf16))
        up_bias = [jnp.sum(pre_grad[z], 0, dtype=f32) for z in range(2)]
        normed_grad = resid_two + core_sum(sum(mt(pre_grad[z], wb[z][:, :HID]) for z in range(2)))
        pieces = plane_pieces(weight_grad([(normed_low, pre_grad), (grad_low, hidden)]))
        if l == 1:
            one = plane_exchange(pieces)
        else:
            one = line_sum(one.reshape(4, 96, HALF).astype(bf16), place).astype(bf16)
            zero = plane_exchange(jnp.concatenate([pieces, one_a.reshape(16, 48, HALF)], 1))
        resid_one, gain_one, shift_one = norm_backward(normed_grad, unit_one, inverse_one, gain[0])
        attn_low = resid_one.astype(bf16)
        out_bias = jnp.sum(attn_low, 0, dtype=f32)
        mixture_grad = jnp.concatenate([mm(attn_low, wa[z][:, 3 * BLOCK :]) for z in range(2)], 1).astype(bf16)
        query_grad, key_grad, value_grad = attend_backward(query, keys, values, probs, mixture_grad)
        key_value_grad = jnp.concatenate([key_grad, value_grad], 1).reshape(4, QUARTER, 4 * BLOCK)
        parts = [swapped(key_value_grad[i].astype(bf16), LINE, 4, bits) for i, bits in ((1, 1), (2, 3), (3, 2))]
        key_value_grad = key_value_grad[0] + sum(part.astype(f32) for part in parts)
        if l == 0:
            key_value_grad = key_value_grad + when(one)
            one = lax.all_gather(one, PLANE, axis=0, tiled=True)
        qkv_grad = []
        for z in range(2):
            cut = slice(z * BLOCK, (z + 1) * BLOCK)
            later = slice((z + 2) * BLOCK, (z + 3) * BLOCK)
            qkv_grad.append(
                jnp.concatenate([query_grad[:, cut], key_value_grad[:, cut], key_value_grad[:, later]], 1).astype(bf16)
            )
        qkv_bias = [jnp.sum(qkv_grad[z], 0, dtype=f32) for z in range(2)]
        grad_state = resid_one + core_sum(sum(mt(qkv_grad[z], wa[z][:, : 3 * BLOCK]) for z in range(2)))
        wide = [out_bias, down_bias, gain_one, gain_two, shift_one, shift_two] + wide
        narrow = [[qkv_bias[z], up_bias[z]] + narrow[z] for z in range(2)]
        pairs_a = [(low, qkv_grad), (attn_low, mix_parts)]
        if l == 1:
            one = plane_sum(one)
            grad_state = grad_state + when(one)
            one_a = line_sum(weight_grad(pairs_a).reshape(4, PACK_A, HALF), place).astype(bf16)
        else:
            wide = jnp.stack(wide)
            small = [
                jnp.concatenate([wide[:, (j // 2) * HALF : (j // 2 + 1) * HALF].reshape(-1)] + narrow[j % 2])
                for j in range(4)
            ]
            small = split3(jnp.stack(small).reshape(4, SMALL, HALF)).transpose(1, 0, 2, 3).reshape(4, 3 * SMALL, HALF)
            small = jnp.pad(small, ((0, 0), (0, 64 - 3 * SMALL), (0, 0)))
            zero_a = line_sum(weight_grad(pairs_a, small).reshape(4, PACK_A + 64, HALF), place)
            zero = plane_sum(zero) + when(one)

    grad_in = to_output(grad_state)

    small = jnp.sum(zero_a[PACK_A : PACK_A + 3 * SMALL].reshape(3, SMALL, HALF), 0)
    small = split3(jnp.pad(small, ((0, 32 - SMALL), (0, 0))))
    small = small.reshape(3, 16, 2, HALF).transpose(1, 0, 2, 3).reshape(16, 6, HALF)
    zero_a = (zero_a[:PACK_A] + when(zero)).astype(bf16).reshape(16, 48, HALF)
    moved = plane_exchange(jnp.concatenate([zero_a, small, jnp.zeros((16, 2, HALF), bf16)], 1))
    zero_b = line_sum(zero[:HALF].reshape(4, 96, HALF).astype(bf16), place).astype(bf16)
    small = split3(jnp.sum(moved[:, 48:54].reshape(48, 2, HALF), 0, dtype=f32)).reshape(6, HALF)
    zero_a = plane_sum(moved[:, :48]).astype(bf16)
    zero = jnp.concatenate([zero_b, zero[HALF:].astype(bf16), zero_a, small, jnp.zeros((2, HALF), bf16)], 0)
    zero = jnp.stack(in_order(near_first(gather(zero, "y")), at_y))
    zero = jnp.stack(in_order(near_first(gather(zero, "x")), at_x)).reshape(16, 200, HALF)
    own = jnp.sum(zero[:, 192:198].reshape(16, 3, 2, HALF), 1, dtype=f32).reshape(32 * HALF)
    wide = own[: 12 * HALF].reshape(LAYERS, 6, HALF)
    own = own[12 * HALF : SMALL * HALF].reshape(LAYERS, 3 * BLOCK + HID)
    grad_a = [zero[:, 144:192].reshape(PACK_A, HALF), zero[:, 96:144].reshape(PACK_A, HALF)]
    grad_b = [zero[:, :96].reshape(PACK_B, HALF), one.reshape(PACK_B, HALF)]

    def both(parts, turn):
        return jnp.stack([part.T if turn else part for part in parts]).astype(f32)

    return (
        output,
        grad_in,
        both([part[: 3 * BLOCK] for part in grad_a], True).reshape(LAYERS, HALF, 3, BLOCK),
        jnp.stack([own[:, :BLOCK], own[:, 2 * BLOCK : 3 * BLOCK]], 1),
        both([part[3 * BLOCK :] for part in grad_a], False),
        wide[:, 0],
        both([part[:HID] for part in grad_b], True),
        own[:, 3 * BLOCK :],
        both([part[HID:] for part in grad_b], False),
        wide[:, 1],
        wide[:, 2:4],
        wide[:, 4:6],
    )


def solution(mesh):
    fine = Mesh(mesh.devices.reshape(4, 4, 2, 2, 2), ("x", "y", "row", "zl", "core"))
    tokens = P(("x", "y", "zl", "core"), "row")
    col = ("zl", "core")
    in_specs = (
        tokens,
        tokens,
        P(("x", "y")),
        P(None, "row", None, col),
        P(None, None, col),
        P(None, col, "row"),
        P(None, "row"),
        P(None, "row", col),
        P(None, col),
        P(None, col, "row"),
        P(None, "row"),
        P(None, None, "row"),
        P(None, None, "row"),
    )
    out_specs = (tokens, tokens) + in_specs[3:8] + (in_specs[8],) + in_specs[9:11] + (in_specs[11], in_specs[12])
    return jax.shard_map(on_device, mesh=fine, in_specs=in_specs, out_specs=out_specs, check_vma=False)
```
